32 devices in a mesh: shot: 2 (over y), freq: 8 (over z, x), field: 2 (over core).
Axes of the slice: x: 2, y: 2, z: 4, core: 2. Of those that a mesh axis runs over, the one named last changes fastest.
Arguments:
- traces: bfloat16 [2, 1024, 32, 256], P('field', None, ('shot', 'freq')), parts along dimension 2, may hold values from -6 to 6
- slowness: float32 [4, 16, 256], P('shot', 'freq'), parts along dimension 0, may hold values from 0.4 to 1
Outputs:
- image: float32 [32, 2, 16, 256], P(('shot', 'freq'), None, 'field'), parts along dimension 0
The draws below stay inside these ranges and needn't reach their ends.
There are 2 independent parts, one for each index of `shot`. The reference program is written for one: setup_inputs(seed, part) draws one part's arguments, and reference() takes and returns one part's arrays. A program takes and returns all parts, laid end to end along the dimension named above; each array names one. Nothing has to cross between parts.
All inputs are finite; a program needn't handle non-finite values.
Results may differ from the reference program's by a relative error of at most 0.0032.
Values sent between devices are 32-bit elements; how exact they have to be, the bound alone decides.
A program may use at most 64 MiB of HBM per device.

```python
import math
import jax
import jax.numpy as jnp
from jax import lax

NT = 1024
NY = 256
DEPTHS = 2
NTERMS = 12
NODES = 16
NF = 16
NX = 16


def steps_of(key, dims, pieces, least, top_value):
    def one(axis_at, parts):
        draws = jax.random.uniform(jax.random.fold_in(jax.random.fold_in(key, 6), axis_at), (parts,), jnp.float32, least / len(pieces), top_value / len(pieces))
        return jnp.repeat(jnp.exp(draws), dims[axis_at] // parts).reshape((-1,) + (1,) * (len(dims) - axis_at - 1))

    level = one(*pieces[0])
    for cut in pieces[1:]:
        level = level * one(*cut)
    return level


def gaussian(key, shape, spread, most, pieces=(), kind=jnp.bfloat16):
    factor_of = steps_of(key, shape, pieces, -0.22, 0.18) if pieces else 1.0
    entries = jax.random.normal(key, shape, jnp.float32) * spread * factor_of
    return jnp.minimum(jnp.maximum(entries, -most), most).astype(kind)


def setup_inputs(seed: int = 0, part: int = 0) -> dict:
    streams_of = jax.random.split(jax.random.key(seed), 3)
    part_keys = jax.random.split(jax.random.fold_in(streams_of[2], part), 3)
    traces = gaussian(part_keys[0], (2, NT, NX, NY), 1.0, 6.0, ((0, 2), (2, 8)))
    slowness = jnp.clip(0.4 + 0.6 * jax.random.uniform(part_keys[1], (DEPTHS, NX, NY), jnp.float32) ** steps_of(part_keys[1], (DEPTHS, NX, NY), ((1, 8),), -0.2, 0.2), 0.4, 1.0)
    return {"traces": traces, "slowness": slowness}


lowest_bin = 8
top_wavenumber = 3.0

def dft_table(bin_count, length):
    freq_bins = lowest_bin + jnp.arange(bin_count, dtype=jnp.int32)
    samples = jnp.arange(length, dtype=jnp.int32)
    phases = freq_bins[:, None] * samples[None, :] % length
    angles = phases.astype(jnp.float32) * (2.0 * math.pi / length)
    norm_scale = 1.0 / math.sqrt(length)
    return jnp.concatenate([jnp.cos(angles) * norm_scale, -jnp.sin(angles) * norm_scale], axis=0).astype(jnp.bfloat16)

def coefficients(slow_plane, freq_bins, bin_count):
    node_angles = (jnp.arange(NODES, dtype=jnp.float32) + 0.5) * (math.pi / NODES)
    term_order = jnp.arange(NTERMS, dtype=jnp.float32)
    weights = jnp.cos(node_angles[:, None] * term_order[None, :]) * (2.0 / NODES)
    weights = weights * jnp.where(term_order == 0, 0.5, 1.0)[None, :]
    wavenumber = top_wavenumber * freq_bins[:, None, None] / (lowest_bin + bin_count) * slow_plane[None]
    depart = wavenumber[None] ** 2 - (node_angles ** 2)[:, None, None, None]
    travel = jnp.sqrt(jnp.maximum(depart, 0.0))
    amplitude = jnp.exp(-jnp.sqrt(jnp.maximum(-depart, 0.0)))
    real_part = amplitude * jnp.cos(travel)
    imag_part = amplitude * jnp.sin(travel)
    real_coef = jnp.einsum('jn,jfxy->nfxy', weights, real_part, precision=lax.Precision.HIGHEST)
    imag_coef = jnp.einsum('jn,jfxy->nfxy', weights, imag_part, precision=lax.Precision.HIGHEST)
    return (real_coef, imag_coef)

def shift_rows(values):
    padded = jnp.pad(values, [(0, 0)] * (values.ndim - 2) + [(1, 1), (0, 0)])
    return 0.5 * (padded[..., 2:, :] + padded[..., :-2, :])

def shift_cols(values):
    padded = jnp.pad(values, [(0, 0)] * (values.ndim - 1) + [(1, 1)])
    return 0.5 * (padded[..., 2:] + padded[..., :-2])

def lateral(values):
    along_rows = shift_rows(values)
    return 0.5 * (along_rows + shift_cols(values) + shift_cols(along_rows) - values)

def extrapolate(wavefield, real_coef, imag_coef, conj_sign):

    def add_term(summed, term_field, position):
        real_c = lax.dynamic_index_in_dim(real_coef, position, 0, keepdims=False)
        imag_c = conj_sign * lax.dynamic_index_in_dim(imag_coef, position, 0, keepdims=False)
        product = jnp.stack([real_c * term_field[0] - imag_c * term_field[1], real_c * term_field[1] + imag_c * term_field[0]])
        return summed + product
    first_term = lateral(wavefield)
    summed = add_term(jnp.zeros_like(wavefield), wavefield, 0)
    summed = add_term(summed, first_term, 1)

    def advance(position, state):
        previous, current, summed = state
        following = 2.0 * lateral(current) - previous
        return (current, following, add_term(summed, following, position))
    state = lax.fori_loop(2, NTERMS, advance, (wavefield, first_term, summed))
    return state[2]

def reference(traces, slowness):
    dft_rows = dft_table(NF, NT)

    def spectra_of(which):
        flat_traces = traces[which].reshape(NT, NX * NY)
        return jnp.dot(dft_rows, flat_traces, preferred_element_type=jnp.float32).reshape(2, NF, NX, NY)
    source_all = spectra_of(0)
    receiver_all = spectra_of(1)

    def one_freq(freq_pos):
        freq_bins = (lowest_bin + freq_pos).astype(jnp.float32)[None]
        source_field = lax.dynamic_index_in_dim(source_all, freq_pos, 1, keepdims=True)
        receiver_field = lax.dynamic_index_in_dim(receiver_all, freq_pos, 1, keepdims=True)
        images = []
        for depth_step in range(DEPTHS):
            real_coef, imag_coef = coefficients(slowness[depth_step], freq_bins, NF)
            source_field = extrapolate(source_field, real_coef, imag_coef, 1.0)
            receiver_field = extrapolate(receiver_field, real_coef, imag_coef, -1.0)
            images.append(source_field[0, 0] * receiver_field[0, 0] + source_field[1, 0] * receiver_field[1, 0])
        return jnp.stack(images)
    return lax.map(one_freq, jnp.arange(NF, dtype=jnp.int32))
```

```python
import functools
import math

import jax
import jax.numpy as jnp
import numpy as np
from jax import lax
from jax.experimental import pallas as pl
from jax.experimental.pallas import tpu as pltpu
from jax.sharding import PartitionSpec as P

NTERMS = 12
NODES = 16
LANES = 128
SUBLANES = 8

lowest_bin = 8
top_wavenumber = 3.0


def dft_rows(bin_count, length, peers, cores, rows_here):
    bins = lowest_bin + np.arange(bin_count)
    samples = np.arange(length)
    angles = (bins[:, None] * samples[None, :] % length).astype(np.float64) * (2.0 * math.pi / length)
    norm_scale = 1.0 / math.sqrt(length)
    table = np.stack([np.cos(angles) * norm_scale, -np.sin(angles) * norm_scale], axis=1)
    table = table.astype(np.float32).astype(jnp.bfloat16)
    spread = np.zeros((bin_count, 2, rows_here, length, rows_here), dtype=jnp.bfloat16)
    for row in range(rows_here):
        spread[:, :, row, :, row] = table
    return spread.reshape(bin_count * 2 * rows_here, length * rows_here)


def power_series(function, degree):
    reach = top_wavenumber**2
    nodes = 0.5 * reach * (1.0 + np.cos(np.pi * (np.arange(64) + 0.5) / 64))
    fitted = np.polynomial.Chebyshev.fit(nodes, function(np.sqrt(nodes)), degree, domain=[0.0, reach])
    return [float(c) for c in fitted.convert(kind=np.polynomial.Polynomial).coef]


COS_SERIES = power_series(np.cos, 6)
SINC_SERIES = power_series(lambda s: np.sin(s) / s, 5)
NODE_ANGLES = [math.pi * (j + 0.5) / NODES for j in range(NODES)]


def horner(series, at):
    value = series[-1] * at + series[-2]
    for factor in series[-3::-1]:
        value = value * at + factor
    return value


def node_value(squared, angle):
    depart = squared - angle * angle
    size = jnp.maximum(jnp.abs(depart), 1e-30)
    root = size * lax.rsqrt(size)
    travels = depart >= 0.0
    real_part = jnp.where(travels, horner(COS_SERIES, depart), jnp.exp(-root))
    imag_part = jnp.where(travels, root * horner(SINC_SERIES, depart), 0.0)
    return real_part, imag_part


def weight(term, node):
    return math.cos(term * NODE_ANGLES[node]) * 2.0 / NODES * (0.5 if term == 0 else 1.0)


def project(parts, terms, count):
    if count > 2:
        half = count // 2
        sums = [parts[j] + parts[count - 1 - j] for j in range(half)]
        stride = NODES // count
        even = [t for t in terms if (t // stride) % 2 == 0]
        odd = [t for t in terms if (t // stride) % 2 == 1]
        found = project(sums, even, half)
        diffs = [parts[j] - parts[count - 1 - j] for j in range(half)]
        for t in odd:
            found[t] = functools.reduce(
                lambda a, b: a + b, [diffs[j] * weight(t, j) for j in range(half)]
            )
        return found
    return {
        t: functools.reduce(lambda a, b: a + b, [parts[j] * weight(t, j) for j in range(count)])
        for t in terms
    }


def lane_pair_sum(values, lane):
    zero = jnp.zeros_like(values[:, :, :1])
    right = pltpu.roll(values, 1, 4)
    left = pltpu.roll(values, LANES - 1, 4)
    from_left = jnp.where(lane == 0, jnp.concatenate([zero, right[:, :, :-1]], axis=2), right)
    from_right = jnp.where(lane == LANES - 1, jnp.concatenate([left[:, :, 1:], zero], axis=2), left)
    return from_left + from_right


def row_pair_sum(values, row):
    zero = jnp.zeros_like(values[:, :1])
    down = pltpu.roll(values, 1, 3)
    up = pltpu.roll(values, SUBLANES - 1, 3)
    from_above = jnp.where(row == 0, jnp.concatenate([zero, down[:, :-1]], axis=1), down)
    from_below = jnp.where(row == SUBLANES - 1, jnp.concatenate([up[:, 1:], zero], axis=1), up)
    return from_above + from_below


def spread_twice(values, lane, row):
    along = values + 0.5 * lane_pair_sum(values, lane)
    return along + 0.5 * row_pair_sum(along, row)


def kernel(
    peers, cores, depths, rows_here, bin_count, cols,
    traces_ref, table_ref, slow_ref, out_ref,
    traces_v, table_v, own_slow, all_slow, send, recv, slow_t, coef, field, image,
    load_sem, slow_send, slow_recv, spec_send, spec_recv, image_send, image_recv,
):
    me = lax.axis_index("freq")
    core = lax.axis_index("field")
    groups = peers * rows_here // SUBLANES
    tiles = cols // LANES
    chunks = groups * tiles

    barrier = pltpu.get_barrier_semaphore()
    others = [(off, turn) for off in range(peers) for turn in range(cores) if (off, turn) != (0, 0)]
    for off, turn in others:
        pl.semaphore_signal(
            barrier, inc=1,
            device_id={"freq": lax.rem(me + off, peers), "field": lax.rem(core + turn, cores)},
            device_id_type=pl.DeviceIdType.MESH,
        )
    load_slow = pltpu.make_async_copy(slow_ref, own_slow, load_sem.at[0])
    load_slow.start()
    load_table = pltpu.make_async_copy(table_ref, table_v, load_sem.at[1])
    load_table.start()
    loads = []
    for t in range(tiles):
        load = pltpu.make_async_copy(
            traces_ref.at[:, :, pl.ds(t * LANES, LANES)], traces_v.at[t], load_sem.at[2 + t]
        )
        load.start()
        loads.append(load)
    load_slow.wait()
    pl.semaphore_wait(barrier, len(others))

    slow_copies = []
    for off in range(1, peers):
        copy = pltpu.make_async_remote_copy(
            src_ref=own_slow, dst_ref=all_slow.at[me],
            send_sem=slow_send.at[off], recv_sem=slow_recv.at[off],
            device_id={"freq": lax.rem(me + off, peers)}, device_id_type=pl.DeviceIdType.MESH,
        )
        copy.start()
        slow_copies.append(copy)
    all_slow[me] = own_slow[...]

    load_table.wait()
    length = traces_v.shape[1]
    for t in range(tiles):
        loads[t].wait()
        block = traces_v[t].reshape(length * rows_here, LANES)
        part = jnp.dot(table_v[...], block, preferred_element_type=jnp.float32)
        send[:, :, :, t * LANES : (t + 1) * LANES] = part.reshape(peers, cores, 2 * rows_here, LANES)

    spec_copies = []
    for number, (off, turn) in enumerate(others):
        peer, side = lax.rem(me + off, peers), lax.rem(core + turn, cores)
        copy = pltpu.make_async_remote_copy(
            src_ref=send.at[peer, side], dst_ref=recv.at[core, me],
            send_sem=spec_send.at[number], recv_sem=spec_recv.at[number],
            device_id={"freq": peer, "field": side}, device_id_type=pl.DeviceIdType.MESH,
        )
        copy.start()
        spec_copies.append(copy)
    recv[core, me] = send[me, core]

    for copy in slow_copies:
        copy.wait()
    for z in range(depths):
        for p in range(peers):
            group, inner = divmod(p * rows_here, SUBLANES)
            for t in range(tiles):
                slow_t[z * chunks + group * tiles + t, inner : inner + rows_here, :] = all_slow[
                    p, z, :, t * LANES : (t + 1) * LANES
                ]

    bin_here = (lowest_bin + me * cores + core).astype(jnp.float32)
    per_slow = top_wavenumber * bin_here / (lowest_bin + bin_count)

    def coefficients(chunk, carry):
        wavenumber = per_slow * slow_t[chunk]
        squared = wavenumber * wavenumber
        pairs = [node_value(squared, angle) for angle in NODE_ANGLES]
        for comp in range(2):
            found = project([pair[comp] for pair in pairs], list(range(NTERMS)), NODES)
            for term in range(NTERMS):
                coef[chunk, 2 * term + comp] = found[term]
        return carry

    lax.fori_loop(0, depths * chunks, coefficients, 0)

    for copy in spec_copies:
        copy.wait()
    for s in range(cores):
        for p in range(peers):
            group, inner = divmod(p * rows_here, SUBLANES)
            for c in range(2):
                for t in range(tiles):
                    field[2 * s + c, group, t, inner : inner + rows_here, :] = recv[
                        s, p, c * rows_here : (c + 1) * rows_here, t * LANES : (t + 1) * LANES
                    ]

    shape = (1, 1, 1, SUBLANES, LANES)
    lane = lax.broadcasted_iota(jnp.int32, shape, 4)
    row = lax.broadcasted_iota(jnp.int32, shape, 3)
    values = field[...]
    half_groups = groups // 2
    image_copies = []
    for z in range(depths):

        def term_of(current, n):
            here = coef[z * chunks : (z + 1) * chunks, pl.ds(2 * n, 2)]
            real_c = here[:, 0].reshape(groups, tiles, SUBLANES, LANES)
            imag_c = here[:, 1].reshape(groups, tiles, SUBLANES, LANES)
            return jnp.stack(
                [
                    real_c * current[0] - imag_c * current[1],
                    real_c * current[1] + imag_c * current[0],
                    real_c * current[2] + imag_c * current[3],
                    real_c * current[3] - imag_c * current[2],
                ]
            )

        first = 0.5 * spread_twice(values, lane, row) - values
        summed = term_of(values, 0) + term_of(first, 1)

        def advance(n, state):
            previous, current, total = state
            following = spread_twice(current, lane, row) - (2.0 * current + previous)
            return current, following, total + term_of(following, n)

        values = lax.fori_loop(
            2, NTERMS, advance, (values, first, summed), unroll=groups <= 4
        )[2]
        picture = values[0] * values[2] + values[1] * values[3]
        for group in range(groups):
            for t in range(tiles):
                image[z, group // half_groups,
                      (group % half_groups) * SUBLANES : (group % half_groups + 1) * SUBLANES,
                      t * LANES : (t + 1) * LANES] = picture[group, t]
        other = lax.rem(core + 1, cores)
        copy = pltpu.make_async_remote_copy(
            src_ref=image.at[z, other], dst_ref=out_ref.at[core, z],
            send_sem=image_send.at[z], recv_sem=image_recv.at[z],
            device_id={"field": other}, device_id_type=pl.DeviceIdType.MESH,
        )
        copy.start()
        image_copies.append(copy)
        out_ref[core, z] = image[z, core]
    for copy in image_copies:
        copy.wait()


def local(traces, slowness):
    peers, cores = lax.axis_size("freq"), lax.axis_size("field")
    _, length, rows_here, cols = traces.shape
    depths = slowness.shape[0]
    bin_count = peers * cores
    table = jnp.asarray(dft_rows(bin_count, length, peers, cores, rows_here))
    grid_rows = peers * rows_here
    groups, tiles = grid_rows // SUBLANES, cols // LANES
    f32 = jnp.float32
    others = peers * cores - 1
    return pl.pallas_call(
        functools.partial(kernel, peers, cores, depths, rows_here, bin_count, cols),
        out_shape=jax.ShapeDtypeStruct((cores, depths, grid_rows // 2, cols), f32),
        in_specs=[pl.BlockSpec(memory_space=pl.ANY)] * 3,
        out_specs=pl.BlockSpec(memory_space=pltpu.VMEM),
        scratch_shapes=[
            pltpu.VMEM((tiles, length, rows_here, LANES), jnp.bfloat16),
            pltpu.VMEM(table.shape, jnp.bfloat16),
            pltpu.VMEM((depths, rows_here, cols), f32),
            pltpu.VMEM((peers, depths, rows_here, cols), f32),
            pltpu.VMEM((peers, cores, 2 * rows_here, cols), f32),
            pltpu.VMEM((cores, peers, 2 * rows_here, cols), f32),
            pltpu.VMEM((depths * groups * tiles, SUBLANES, LANES), f32),
            pltpu.VMEM((depths * groups * tiles, 2 * NTERMS, SUBLANES, LANES), f32),
            pltpu.VMEM((4, groups, tiles, SUBLANES, LANES), f32),
            pltpu.VMEM((depths, 2, grid_rows // 2, cols), f32),
            pltpu.SemaphoreType.DMA((2 + tiles,)),
            pltpu.SemaphoreType.DMA((peers,)),
            pltpu.SemaphoreType.DMA((peers,)),
            pltpu.SemaphoreType.DMA((others,)),
            pltpu.SemaphoreType.DMA((others,)),
            pltpu.SemaphoreType.DMA((depths,)),
            pltpu.SemaphoreType.DMA((depths,)),
        ],
        compiler_params=pltpu.CompilerParams(
            collective_id=0, has_side_effects=True, vmem_limit_bytes=48 * 1024 * 1024
        ),
    )(traces[0], table, slowness)


def solution(mesh):
    return jax.shard_map(
        local,
        mesh=mesh,
        in_specs=(P("field", None, ("shot", "freq"), None), P("shot", "freq", None)),
        out_specs=P(("shot", "freq"), None, "field", None),
        check_vma=False,
    )
```

```python
import functools
import math

import jax
import jax.numpy as jnp
import numpy as np
from jax import lax
from jax.experimental import pallas as pl
from jax.experimental.pallas import tpu as pltpu
from jax.sharding import PartitionSpec as P

NTERMS = 12
NODES = 16
LANES = 128
SUBLANES = 8

lowest_bin = 8
top_wavenumber = 3.0


def dft_rows(bin_count, length, peers, cores, rows_here):
    bins = lowest_bin + np.arange(bin_count)
    samples = np.arange(length)
    angles = (bins[:, None] * samples[None, :] % length).astype(np.float64) * (2.0 * math.pi / length)
    norm_scale = 1.0 / math.sqrt(length)
    table = np.stack([np.cos(angles) * norm_scale, -np.sin(angles) * norm_scale], axis=1)
    table = table.astype(np.float32).astype(jnp.bfloat16)
    spread = np.zeros((bin_count, 2, rows_here, length, rows_here), dtype=jnp.bfloat16)
    for row in range(rows_here):
        spread[:, :, row, :, row] = table
    return spread.reshape(bin_count * 2 * rows_here, length * rows_here)


def power_series(function, degree):
    reach = top_wavenumber**2
    nodes = 0.5 * reach * (1.0 + np.cos(np.pi * (np.arange(64) + 0.5) / 64))
    fitted = np.polynomial.Chebyshev.fit(nodes, function(np.sqrt(nodes)), degree, domain=[0.0, reach])
    return [float(c) for c in fitted.convert(kind=np.polynomial.Polynomial).coef]


COS_SERIES = power_series(np.cos, 6)
SINC_SERIES = power_series(lambda s: np.sin(s) / s, 5)
NODE_ANGLES = [math.pi * (j + 0.5) / NODES for j in range(NODES)]


def horner(series, at):
    value = series[-1] * at + series[-2]
    for factor in series[-3::-1]:
        value = value * at + factor
    return value


def node_value(squared, angle):
    depart = squared - angle * angle
    size = jnp.maximum(jnp.abs(depart), 1e-30)
    root = size * lax.rsqrt(size)
    travels = depart >= 0.0
    real_part = jnp.where(travels, horner(COS_SERIES, depart), jnp.exp(-root))
    imag_part = jnp.where(travels, root * horner(SINC_SERIES, depart), 0.0)
    return real_part, imag_part


def weight(term, node):
    return math.cos(term * NODE_ANGLES[node]) * 2.0 / NODES * (0.5 if term == 0 else 1.0)


def project(parts, terms, count):
    if count > 2:
        half = count // 2
        sums = [parts[j] + parts[count - 1 - j] for j in range(half)]
        stride = NODES // count
        even = [t for t in terms if (t // stride) % 2 == 0]
        odd = [t for t in terms if (t // stride) % 2 == 1]
        found = project(sums, even, half)
        diffs = [parts[j] - parts[count - 1 - j] for j in range(half)]
        for t in odd:
            found[t] = functools.reduce(
                lambda a, b: a + b, [diffs[j] * weight(t, j) for j in range(half)]
            )
        return found
    return {
        t: functools.reduce(lambda a, b: a + b, [parts[j] * weight(t, j) for j in range(count)])
        for t in terms
    }


def lane_pair_sum(values, lane):
    zero = jnp.zeros_like(values[:, :, :1])
    right = pltpu.roll(values, 1, 4)
    left = pltpu.roll(values, LANES - 1, 4)
    from_left = jnp.where(lane == 0, jnp.concatenate([zero, right[:, :, :-1]], axis=2), right)
    from_right = jnp.where(lane == LANES - 1, jnp.concatenate([left[:, :, 1:], zero], axis=2), left)
    return from_left + from_right


def row_pair_sum(values, row):
    zero = jnp.zeros_like(values[:, :1])
    down = pltpu.roll(values, 1, 3)
    up = pltpu.roll(values, SUBLANES - 1, 3)
    from_above = jnp.where(row == 0, jnp.concatenate([zero, down[:, :-1]], axis=1), down)
    from_below = jnp.where(row == SUBLANES - 1, jnp.concatenate([up[:, 1:], zero], axis=1), up)
    return from_above + from_below


def spread_twice(values, lane, row):
    along = values + 0.5 * lane_pair_sum(values, lane)
    return along + 0.5 * row_pair_sum(along, row)


def kernel(
    peers, cores, depths, rows_here, bin_count, cols,
    traces_ref, table_ref, slow_ref, out_ref,
    traces_v, table_v, own_slow, all_slow, send, recv, slow_t, coef, field, image,
    load_sem, slow_send, slow_recv, spec_send, spec_recv, image_send, image_recv,
):
    me = lax.axis_index("freq")
    core = lax.axis_index("field")
    groups = peers * rows_here // SUBLANES
    tiles = cols // LANES
    chunks = groups * tiles

    barrier = pltpu.get_barrier_semaphore()
    others = [(off, turn) for off in range(peers) for turn in range(cores) if (off, turn) != (0, 0)]
    for off, turn in others:
        pl.semaphore_signal(
            barrier, inc=1,
            device_id={"freq": lax.rem(me + off, peers), "field": lax.rem(core + turn, cores)},
            device_id_type=pl.DeviceIdType.MESH,
        )
    load_slow = pltpu.make_async_copy(slow_ref, own_slow, load_sem.at[0])
    load_slow.start()
    load_table = pltpu.make_async_copy(table_ref, table_v, load_sem.at[1])
    load_table.start()
    loads = []
    for t in range(tiles):
        load = pltpu.make_async_copy(
            traces_ref.at[:, :, pl.ds(t * LANES, LANES)], traces_v.at[t], load_sem.at[2 + t]
        )
        load.start()
        loads.append(load)
    load_slow.wait()
    pl.semaphore_wait(barrier, len(others))

    slow_copies = []
    for off in range(1, peers):
        copy = pltpu.make_async_remote_copy(
            src_ref=own_slow, dst_ref=all_slow.at[me],
            send_sem=slow_send.at[off], recv_sem=slow_recv.at[off],
            device_id={"freq": lax.rem(me + off, peers)}, device_id_type=pl.DeviceIdType.MESH,
        )
        copy.start()
        slow_copies.append(copy)
    all_slow[me] = own_slow[...]

    load_table.wait()
    length = traces_v.shape[1]
    for t in range(tiles):
        loads[t].wait()
        block = traces_v[t].reshape(length * rows_here, LANES)
        part = jnp.dot(table_v[...], block, preferred_element_type=jnp.float32)
        send[:, :, :, t * LANES : (t + 1) * LANES] = part.reshape(peers, cores, 2 * rows_here, LANES)

    spec_copies = []
    for number, (off, turn) in enumerate(others):
        peer, side = lax.rem(me + off, peers), lax.rem(core + turn, cores)
        copy = pltpu.make_async_remote_copy(
            src_ref=send.at[peer, side], dst_ref=recv.at[core, me],
            send_sem=spec_send.at[number], recv_sem=spec_recv.at[number],
            device_id={"freq": peer, "field": side}, device_id_type=pl.DeviceIdType.MESH,
        )
        copy.start()
        spec_copies.append(copy)
    recv[core, me] = send[me, core]

    for copy in slow_copies:
        copy.wait()
    for z in range(depths):
        for p in range(peers):
            group, inner = divmod(p * rows_here, SUBLANES)
            for t in range(tiles):
                slow_t[z * chunks + group * tiles + t, inner : inner + rows_here, :] = all_slow[
                    p, z, :, t * LANES : (t + 1) * LANES
                ]

    bin_here = (lowest_bin + me * cores + core).astype(jnp.float32)
    per_slow = top_wavenumber * bin_here / (lowest_bin + bin_count)

    def coefficients(chunk, carry):
        wavenumber = per_slow * slow_t[chunk]
        squared = wavenumber * wavenumber
        pairs = [node_value(squared, angle) for angle in NODE_ANGLES]
        for comp in range(2):
            found = project([pair[comp] for pair in pairs], list(range(NTERMS)), NODES)
            for term in range(NTERMS):
                coef[chunk, 2 * term + comp] = found[term]
        return carry

    lax.fori_loop(0, depths * chunks, coefficients, 0)

    for copy in spec_copies:
        copy.wait()
    for s in range(cores):
        for p in range(peers):
            group, inner = divmod(p * rows_here, SUBLANES)
            for c in range(2):
                for t in range(tiles):
                    field[2 * s + c, group, t, inner : inner + rows_here, :] = recv[
                        s, p, c * rows_here : (c + 1) * rows_here, t * LANES : (t + 1) * LANES
                    ]

    shape = (1, 1, 1, SUBLANES, LANES)
    lane = lax.broadcasted_iota(jnp.int32, shape, 4)
    row = lax.broadcasted_iota(jnp.int32, shape, 3)
    values = field[...]
    half_groups = groups // 2
    image_copies = []
    for z in range(depths):

        def term_of(current, n):
            here = coef[z * chunks : (z + 1) * chunks, pl.ds(2 * n, 2)]
            real_c = here[:, 0].reshape(groups, tiles, SUBLANES, LANES)
            imag_c = here[:, 1].reshape(groups, tiles, SUBLANES, LANES)
            return jnp.stack(
                [
                    real_c * current[0] - imag_c * current[1],
                    real_c * current[1] + imag_c * current[0],
                    real_c * current[2] + imag_c * current[3],
                    real_c * current[3] - imag_c * current[2],
                ]
            )

        first = 0.5 * spread_twice(values, lane, row) - values
        summed = term_of(values, 0) + term_of(first, 1)

        def advance(n, state):
            previous, current, total = state
            following = spread_twice(current, lane, row) - (2.0 * current + previous)
            return current, following, total + term_of(following, n)

        values = lax.fori_loop(
            2, NTERMS, advance, (values, first, summed), unroll=groups <= 4
        )[2]
        picture = values[0] * values[2] + values[1] * values[3]
        for group in range(groups):
            for t in range(tiles):
                image[z, group // half_groups,
                      (group % half_groups) * SUBLANES : (group % half_groups + 1) * SUBLANES,
                      t * LANES : (t + 1) * LANES] = picture[group, t]
        other = lax.rem(core + 1, cores)
        copy = pltpu.make_async_remote_copy(
            src_ref=image.at[z, other], dst_ref=out_ref.at[core, z],
            send_sem=image_send.at[z], recv_sem=image_recv.at[z],
            device_id={"field": other}, device_id_type=pl.DeviceIdType.MESH,
        )
        copy.start()
        image_copies.append(copy)
        out_ref[core, z] = image[z, core]
    for copy in image_copies:
        copy.wait()


def local(traces, slowness):
    peers, cores = lax.axis_size("freq"), lax.axis_size("field")
    _, length, rows_here, cols = traces.shape
    depths = slowness.shape[0]
    bin_count = peers * cores
    table = jnp.asarray(dft_rows(bin_count, length, peers, cores, rows_here))
    grid_rows = peers * rows_here
    groups, tiles = grid_rows // SUBLANES, cols // LANES
    f32 = jnp.float32
    others = peers * cores - 1
    return pl.pallas_call(
        functools.partial(kernel, peers, cores, depths, rows_here, bin_count, cols),
        out_shape=jax.ShapeDtypeStruct((cores, depths, grid_rows // 2, cols), f32),
        in_specs=[pl.BlockSpec(memory_space=pltpu.HBM)] * 3,
        out_specs=pl.BlockSpec(memory_space=pltpu.VMEM),
        scratch_shapes=[
            pltpu.VMEM((tiles, length, rows_here, LANES), jnp.bfloat16),
            pltpu.VMEM(table.shape, jnp.bfloat16),
            pltpu.VMEM((depths, rows_here, cols), f32),
            pltpu.VMEM((peers, depths, rows_here, cols), f32),
            pltpu.VMEM((peers, cores, 2 * rows_here, cols), f32),
            pltpu.VMEM((cores, peers, 2 * rows_here, cols), f32),
            pltpu.VMEM((depths * groups * tiles, SUBLANES, LANES), f32),
            pltpu.VMEM((depths * groups * tiles, 2 * NTERMS, SUBLANES, LANES), f32),
            pltpu.VMEM((4, groups, tiles, SUBLANES, LANES), f32),
            pltpu.VMEM((depths, 2, grid_rows // 2, cols), f32),
            pltpu.SemaphoreType.DMA((2 + tiles,)),
            pltpu.SemaphoreType.DMA((peers,)),
            pltpu.SemaphoreType.DMA((peers,)),
            pltpu.SemaphoreType.DMA((others,)),
            pltpu.SemaphoreType.DMA((others,)),
            pltpu.SemaphoreType.DMA((depths,)),
            pltpu.SemaphoreType.DMA((depths,)),
        ],
        compiler_params=pltpu.CompilerParams(
            collective_id=0, has_side_effects=True, vmem_limit_bytes=64 * 1024 * 1024
        ),
    )(traces[0], table, slowness)


def solution(mesh):
    return jax.shard_map(
        local,
        mesh=mesh,
        in_specs=(P("field", None, ("shot", "freq"), None), P("shot", "freq", None)),
        out_specs=P(("shot", "freq"), None, "field", None),
        check_vma=False,
    )
```

```python
import functools
import math

import jax
import jax.numpy as jnp
import numpy as np
from jax import lax
from jax.experimental import pallas as pl
from jax.experimental.pallas import tpu as pltpu
from jax.sharding import PartitionSpec as P

NTERMS = 12
NODES = 16
LANES = 128
SUBLANES = 8

lowest_bin = 8
top_wavenumber = 3.0


def dft_rows(bin_count, length, peers, cores, rows_here):
    bins = lowest_bin + np.arange(bin_count)
    samples = np.arange(length)
    angles = (bins[:, None] * samples[None, :] % length).astype(np.float64) * (2.0 * math.pi / length)
    norm_scale = 1.0 / math.sqrt(length)
    table = np.stack([np.cos(angles) * norm_scale, -np.sin(angles) * norm_scale], axis=1)
    table = table.astype(np.float32).astype(jnp.bfloat16)
    spread = np.zeros((bin_count, 2, rows_here, length, rows_here), dtype=jnp.bfloat16)
    for row in range(rows_here):
        spread[:, :, row, :, row] = table
    return spread.reshape(bin_count * 2 * rows_here, length * rows_here)


def power_series(function, degree):
    reach = top_wavenumber**2
    nodes = 0.5 * reach * (1.0 + np.cos(np.pi * (np.arange(64) + 0.5) / 64))
    fitted = np.polynomial.Chebyshev.fit(nodes, function(np.sqrt(nodes)), degree, domain=[0.0, reach])
    return [float(c) for c in fitted.convert(kind=np.polynomial.Polynomial).coef]


COS_SERIES = power_series(np.cos, 6)
SINC_SERIES = power_series(lambda s: np.sin(s) / s, 5)
NODE_ANGLES = [math.pi * (j + 0.5) / NODES for j in range(NODES)]


def horner(series, at):
    value = series[-1] * at + series[-2]
    for factor in series[-3::-1]:
        value = value * at + factor
    return value


def node_value(squared, angle):
    depart = squared - angle * angle
    size = jnp.maximum(jnp.abs(depart), 1e-30)
    root = size * lax.rsqrt(size)
    travels = depart >= 0.0
    real_part = jnp.where(travels, horner(COS_SERIES, depart), jnp.exp(-root))
    imag_part = jnp.where(travels, root * horner(SINC_SERIES, depart), 0.0)
    return real_part, imag_part


def weight(term, node):
    return math.cos(term * NODE_ANGLES[node]) * 2.0 / NODES * (0.5 if term == 0 else 1.0)


def project(parts, terms, count):
    if count > 2:
        half = count // 2
        sums = [parts[j] + parts[count - 1 - j] for j in range(half)]
        stride = NODES // count
        even = [t for t in terms if (t // stride) % 2 == 0]
        odd = [t for t in terms if (t // stride) % 2 == 1]
        found = project(sums, even, half)
        diffs = [parts[j] - parts[count - 1 - j] for j in range(half)]
        for t in odd:
            found[t] = functools.reduce(
                lambda a, b: a + b, [diffs[j] * weight(t, j) for j in range(half)]
            )
        return found
    return {
        t: functools.reduce(lambda a, b: a + b, [parts[j] * weight(t, j) for j in range(count)])
        for t in terms
    }


def lane_pair_sum(values, lane):
    zero = jnp.zeros_like(values[:, :, :1])
    right = pltpu.roll(values, 1, 4)
    left = pltpu.roll(values, LANES - 1, 4)
    from_left = jnp.where(lane == 0, jnp.concatenate([zero, right[:, :, :-1]], axis=2), right)
    from_right = jnp.where(lane == LANES - 1, jnp.concatenate([left[:, :, 1:], zero], axis=2), left)
    return from_left + from_right


def row_pair_sum(values, row):
    zero = jnp.zeros_like(values[:, :1])
    down = pltpu.roll(values, 1, 3)
    up = pltpu.roll(values, SUBLANES - 1, 3)
    from_above = jnp.where(row == 0, jnp.concatenate([zero, down[:, :-1]], axis=1), down)
    from_below = jnp.where(row == SUBLANES - 1, jnp.concatenate([up[:, 1:], zero], axis=1), up)
    return from_above + from_below


def spread_twice(values, lane, row):
    along = values + 0.5 * lane_pair_sum(values, lane)
    return along + 0.5 * row_pair_sum(along, row)


def kernel(
    peers, cores, depths, rows_here, bin_count, cols,
    traces_ref, table_ref, slow_ref, out_ref,
    traces_v, table_v, own_slow, send, recv, slow_t, field, image,
    load_sem, spec_send, spec_recv, image_send, image_recv, *coef,
):
    me = lax.axis_index("freq")
    core = lax.axis_index("field")
    groups = peers * rows_here // SUBLANES
    tiles = cols // LANES
    chunks = groups * tiles
    inline = chunks <= 4
    spec_rows = 2 * rows_here

    barrier = pltpu.get_barrier_semaphore()
    others = [(off, turn) for off in range(peers) for turn in range(cores) if (off, turn) != (0, 0)]
    for off, turn in others:
        pl.semaphore_signal(
            barrier, inc=1,
            device_id={"freq": lax.rem(me + off, peers), "field": lax.rem(core + turn, cores)},
            device_id_type=pl.DeviceIdType.MESH,
        )
    loads = []
    for t in range(tiles):
        load = pltpu.make_async_copy(
            traces_ref.at[:, :, pl.ds(t * LANES, LANES)], traces_v.at[t], load_sem.at[2 + t]
        )
        load.start()
        loads.append(load)
    load_table = pltpu.make_async_copy(table_ref, table_v, load_sem.at[1])
    load_table.start()
    load_slow = pltpu.make_async_copy(slow_ref, own_slow, load_sem.at[0])
    load_slow.start()

    load_slow.wait()
    slow_rows = own_slow[...].reshape(depths * rows_here, cols)
    tail = jnp.concatenate([jnp.zeros((spec_rows, cols), jnp.float32), slow_rows], axis=0)
    block_row = lax.broadcasted_iota(jnp.int32, (1, 1, 2 * spec_rows, LANES), 2)
    load_table.wait()
    length = traces_v.shape[1]
    for t in range(tiles):
        loads[t].wait()
        block = traces_v[t].reshape(length * rows_here, LANES)
        part = jnp.dot(table_v[...], block, preferred_element_type=jnp.float32)
        part = part.reshape(peers, 1, cores * spec_rows, LANES)
        both = jnp.concatenate([part, pltpu.roll(part, spec_rows, 2)], axis=1)
        here = tail[:, t * LANES : (t + 1) * LANES]
        send[:, :, :, t * LANES : (t + 1) * LANES] = jnp.where(block_row < spec_rows, both, here[None, None])

    pl.semaphore_wait(barrier, len(others))
    spec_copies = []
    for number, (off, turn) in enumerate(others):
        peer, side = lax.rem(me + off, peers), lax.rem(core + turn, cores)
        copy = pltpu.make_async_remote_copy(
            src_ref=send.at[peer, side], dst_ref=recv.at[core, me],
            send_sem=spec_send.at[number], recv_sem=spec_recv.at[number],
            device_id={"freq": peer, "field": side}, device_id_type=pl.DeviceIdType.MESH,
        )
        copy.start()
        spec_copies.append(copy)
    recv[core, me] = send[me, core]

    for copy in spec_copies:
        copy.wait_recv()
    for z in range(depths):
        for p in range(peers):
            group, inner = divmod(p * rows_here, SUBLANES)
            first_row = spec_rows + z * rows_here
            for t in range(tiles):
                slow_t[z * chunks + group * tiles + t, inner : inner + rows_here, :] = recv[
                    0, p, first_row : first_row + rows_here, t * LANES : (t + 1) * LANES
                ]
    for s in range(cores):
        for p in range(peers):
            group, inner = divmod(p * rows_here, SUBLANES)
            for c in range(2):
                for t in range(tiles):
                    field[2 * s + c, group, t, inner : inner + rows_here, :] = recv[
                        s, p, c * rows_here : (c + 1) * rows_here, t * LANES : (t + 1) * LANES
                    ]

    bin_here = (lowest_bin + me * cores + core).astype(jnp.float32)
    per_slow = top_wavenumber * bin_here / (lowest_bin + bin_count)

    def coefficients(z, chunk):
        wavenumber = per_slow * slow_t[z * chunks + chunk]
        squared = wavenumber * wavenumber
        pairs = [node_value(squared, angle) for angle in NODE_ANGLES]
        for comp in range(2):
            found = project([pair[comp] for pair in pairs], list(range(NTERMS)), NODES)
            for term in range(NTERMS):
                coef[z][2 * term + comp, chunk] = found[term]

    def all_coefficients(z):
        if inline:
            for chunk in range(chunks):
                coefficients(z, chunk)
        else:
            lax.fori_loop(0, chunks, lambda chunk, carry: coefficients(z, chunk) or carry, 0)

    all_coefficients(0)

    shape = (1, 1, 1, SUBLANES, LANES)
    lane = lax.broadcasted_iota(jnp.int32, shape, 4)
    row = lax.broadcasted_iota(jnp.int32, shape, 3)
    values = field[...]
    half_groups = groups // 2
    image_copies = []
    for z in range(depths):

        def term_of(current, n):
            here = coef[z][pl.ds(2 * n, 2)]
            real_c = here[0].reshape(groups, tiles, SUBLANES, LANES)
            imag_c = here[1].reshape(groups, tiles, SUBLANES, LANES)
            return jnp.stack(
                [
                    real_c * current[0] - imag_c * current[1],
                    real_c * current[1] + imag_c * current[0],
                    real_c * current[2] + imag_c * current[3],
                    real_c * current[3] - imag_c * current[2],
                ]
            )

        first = 0.5 * spread_twice(values, lane, row) - values
        summed = term_of(values, 0) + term_of(first, 1)

        def advance(n, state):
            previous, current, total = state
            following = spread_twice(current, lane, row) - (2.0 * current + previous)
            return current, following, total + term_of(following, n)

        state = (values, first, summed)
        if inline:
            for n in range(2, NTERMS):
                state = advance(n, state)
                if z + 1 < depths and n % 2 == 0 and n // 2 <= chunks:
                    coefficients(z + 1, n // 2 - 1)
        else:
            state = lax.fori_loop(2, NTERMS, advance, state)
            if z + 1 < depths:
                all_coefficients(z + 1)
        values = state[2]
        picture = values[0] * values[2] + values[1] * values[3]
        for group in range(groups):
            for t in range(tiles):
                image[z, group // half_groups,
                      (group % half_groups) * SUBLANES : (group % half_groups + 1) * SUBLANES,
                      t * LANES : (t + 1) * LANES] = picture[group, t]
        other = lax.rem(core + 1, cores)
        copy = pltpu.make_async_remote_copy(
            src_ref=image.at[z, other], dst_ref=out_ref.at[core, z],
            send_sem=image_send.at[z], recv_sem=image_recv.at[z],
            device_id={"field": other}, device_id_type=pl.DeviceIdType.MESH,
        )
        copy.start()
        image_copies.append(copy)
        out_ref[core, z] = image[z, core]
    for copy in spec_copies:
        copy.wait_send()
    for copy in image_copies:
        copy.wait()


def local(traces, slowness):
    peers, cores = lax.axis_size("freq"), lax.axis_size("field")
    _, length, rows_here, cols = traces.shape
    depths = slowness.shape[0]
    bin_count = peers * cores
    table = jnp.asarray(dft_rows(bin_count, length, peers, cores, rows_here))
    grid_rows = peers * rows_here
    groups, tiles = grid_rows // SUBLANES, cols // LANES
    f32 = jnp.float32
    others = peers * cores - 1
    return pl.pallas_call(
        functools.partial(kernel, peers, cores, depths, rows_here, bin_count, cols),
        out_shape=jax.ShapeDtypeStruct((cores, depths, grid_rows // 2, cols), f32),
        in_specs=[pl.BlockSpec(memory_space=pltpu.HBM)] * 3,
        out_specs=pl.BlockSpec(memory_space=pltpu.VMEM),
        scratch_shapes=[
            pltpu.VMEM((tiles, length, rows_here, LANES), jnp.bfloat16),
            pltpu.VMEM(table.shape, jnp.bfloat16),
            pltpu.VMEM((depths, rows_here, cols), f32),
            pltpu.VMEM((peers, cores, (2 + depths) * rows_here, cols), f32),
            pltpu.VMEM((cores, peers, (2 + depths) * rows_here, cols), f32),
            pltpu.VMEM((depths * groups * tiles, SUBLANES, LANES), f32),
            pltpu.VMEM((4, groups, tiles, SUBLANES, LANES), f32),
            pltpu.VMEM((depths, 2, grid_rows // 2, cols), f32),
            pltpu.SemaphoreType.DMA((2 + tiles,)),
            pltpu.SemaphoreType.DMA((others,)),
            pltpu.SemaphoreType.DMA((others,)),
            pltpu.SemaphoreType.DMA((depths,)),
            pltpu.SemaphoreType.DMA((depths,)),
        ]
        + [pltpu.VMEM((2 * NTERMS, groups * tiles, SUBLANES, LANES), f32)] * depths,
        compiler_params=pltpu.CompilerParams(
            collective_id=0, has_side_effects=True, vmem_limit_bytes=64 * 1024 * 1024
        ),
    )(traces[0], table, slowness)


def solution(mesh):
    return jax.shard_map(
        local,
        mesh=mesh,
        in_specs=(P("field", None, ("shot", "freq"), None), P("shot", "freq", None)),
        out_specs=P(("shot", "freq"), None, "field", None),
        check_vma=False,
    )
```

```python
import functools
import math

import jax
import jax.numpy as jnp
import numpy as np
from jax import lax
from jax.experimental import pallas as pl
from jax.experimental.pallas import tpu as pltpu
from jax.sharding import PartitionSpec as P

NTERMS = 12
NODES = 16
LANES = 128
SUBLANES = 8
PIECES = 4

lowest_bin = 8
top_wavenumber = 3.0


def dft_rows(bin_count, length, peers, cores, rows_here):
    bins = lowest_bin + np.arange(bin_count)
    samples = np.arange(length)
    angles = (bins[:, None] * samples[None, :] % length).astype(np.float64) * (2.0 * math.pi / length)
    norm_scale = 1.0 / math.sqrt(length)
    table = np.stack([np.cos(angles) * norm_scale, -np.sin(angles) * norm_scale], axis=1)
    table = table.astype(np.float32).astype(jnp.bfloat16)
    spread = np.zeros((bin_count, 2, rows_here, length, rows_here), dtype=jnp.bfloat16)
    for row in range(rows_here):
        spread[:, :, row, :, row] = table
    return spread.reshape(bin_count * 2 * rows_here, length * rows_here)


def power_series(function, degree):
    reach = top_wavenumber**2
    nodes = 0.5 * reach * (1.0 + np.cos(np.pi * (np.arange(64) + 0.5) / 64))
    fitted = np.polynomial.Chebyshev.fit(nodes, function(np.sqrt(nodes)), degree, domain=[0.0, reach])
    return [float(c) for c in fitted.convert(kind=np.polynomial.Polynomial).coef]


COS_SERIES = power_series(np.cos, 6)
SINC_SERIES = power_series(lambda s: np.sin(s) / s, 5)
NODE_ANGLES = [math.pi * (j + 0.5) / NODES for j in range(NODES)]


def horner(series, at):
    value = series[-1] * at + series[-2]
    for factor in series[-3::-1]:
        value = value * at + factor
    return value


def node_value(squared, angle):
    depart = squared - angle * angle
    size = jnp.maximum(jnp.abs(depart), 1e-30)
    root = size * lax.rsqrt(size)
    travels = depart >= 0.0
    real_part = jnp.where(travels, horner(COS_SERIES, depart), jnp.exp(-root))
    imag_part = jnp.where(travels, root * horner(SINC_SERIES, depart), 0.0)
    return real_part, imag_part


def weight(term, node):
    return math.cos(term * NODE_ANGLES[node]) * 2.0 / NODES * (0.5 if term == 0 else 1.0)


def project(parts, terms, count):
    if count > 2:
        half = count // 2
        sums = [parts[j] + parts[count - 1 - j] for j in range(half)]
        stride = NODES // count
        even = [t for t in terms if (t // stride) % 2 == 0]
        odd = [t for t in terms if (t // stride) % 2 == 1]
        found = project(sums, even, half)
        diffs = [parts[j] - parts[count - 1 - j] for j in range(half)]
        for t in odd:
            found[t] = functools.reduce(
                lambda a, b: a + b, [diffs[j] * weight(t, j) for j in range(half)]
            )
        return found
    return {
        t: functools.reduce(lambda a, b: a + b, [parts[j] * weight(t, j) for j in range(count)])
        for t in terms
    }


def lane_pair_sum(values, lane):
    zero = jnp.zeros_like(values[:, :, :1])
    right = pltpu.roll(values, 1, 4)
    left = pltpu.roll(values, LANES - 1, 4)
    from_left = jnp.where(lane == 0, jnp.concatenate([zero, right[:, :, :-1]], axis=2), right)
    from_right = jnp.where(lane == LANES - 1, jnp.concatenate([left[:, :, 1:], zero], axis=2), left)
    return from_left + from_right


def row_pair_sum(values, row):
    zero = jnp.zeros_like(values[:, :1])
    down = pltpu.roll(values, 1, 3)
    up = pltpu.roll(values, SUBLANES - 1, 3)
    from_above = jnp.where(row == 0, jnp.concatenate([zero, down[:, :-1]], axis=1), down)
    from_below = jnp.where(row == SUBLANES - 1, jnp.concatenate([up[:, 1:], zero], axis=1), up)
    return from_above + from_below


def spread_twice(values, lane, row):
    along = values + 0.5 * lane_pair_sum(values, lane)
    return along + 0.5 * row_pair_sum(along, row)


def kernel(
    peers, cores, depths, rows_here, bin_count, cols,
    traces_ref, table_ref, slow_ref, out_ref,
    traces_v, table_v, own_slow, send, recv, slow_t, field, image,
    load_sem, spec_send, spec_recv, image_send, image_recv, *coef,
):
    me = lax.axis_index("freq")
    core = lax.axis_index("field")
    groups = peers * rows_here // SUBLANES
    tiles = cols // LANES
    chunks = groups * tiles
    inline = chunks <= 4
    spec_rows = 2 * rows_here

    barrier = pltpu.get_barrier_semaphore()
    others = [(off, turn) for off in range(peers) for turn in range(cores) if (off, turn) != (0, 0)]
    for off, turn in others:
        pl.semaphore_signal(
            barrier, inc=1,
            device_id={"freq": lax.rem(me + off, peers), "field": lax.rem(core + turn, cores)},
            device_id_type=pl.DeviceIdType.MESH,
        )
    loads = []
    length = traces_v.shape[0]
    piece = length // PIECES
    for t in range(PIECES):
        span = pl.ds(t * piece, piece)
        load = pltpu.make_async_copy(traces_ref.at[span], traces_v.at[span], load_sem.at[2 + t])
        load.start()
        loads.append(load)
    load_table = pltpu.make_async_copy(table_ref, table_v, load_sem.at[1])
    load_table.start()
    load_slow = pltpu.make_async_copy(slow_ref, own_slow, load_sem.at[0])
    load_slow.start()

    load_slow.wait()
    slow_rows = own_slow[...].reshape(depths * rows_here, cols)
    tail = jnp.concatenate([jnp.zeros((spec_rows, cols), jnp.float32), slow_rows], axis=0)
    block_row = lax.broadcasted_iota(jnp.int32, (1, 1, 2 * spec_rows, cols), 2)
    load_table.wait()
    part = jnp.zeros((bin_count * spec_rows, cols), jnp.float32)
    for t in range(PIECES):
        loads[t].wait()
        width = piece * rows_here
        block = traces_v[t * piece : (t + 1) * piece].reshape(width, cols)
        part = part + jnp.dot(
            table_v[:, t * width : (t + 1) * width], block, preferred_element_type=jnp.float32
        )
    part = part.reshape(peers, 1, cores * spec_rows, cols)
    both = jnp.concatenate([part, pltpu.roll(part, spec_rows, 2)], axis=1)
    send[...] = jnp.where(block_row < spec_rows, both, tail[None, None])

    pl.semaphore_wait(barrier, len(others))
    spec_copies = []
    for number, (off, turn) in enumerate(others):
        peer, side = lax.rem(me + off, peers), lax.rem(core + turn, cores)
        copy = pltpu.make_async_remote_copy(
            src_ref=send.at[peer, side], dst_ref=recv.at[core, me],
            send_sem=spec_send.at[number], recv_sem=spec_recv.at[number],
            device_id={"freq": peer, "field": side}, device_id_type=pl.DeviceIdType.MESH,
        )
        copy.start()
        spec_copies.append(copy)
    recv[core, me] = send[me, core]

    for copy in spec_copies:
        copy.wait_recv()
    for z in range(depths):
        for p in range(peers):
            group, inner = divmod(p * rows_here, SUBLANES)
            first_row = spec_rows + z * rows_here
            for t in range(tiles):
                slow_t[z * chunks + group * tiles + t, inner : inner + rows_here, :] = recv[
                    0, p, first_row : first_row + rows_here, t * LANES : (t + 1) * LANES
                ]
    for s in range(cores):
        for p in range(peers):
            group, inner = divmod(p * rows_here, SUBLANES)
            for c in range(2):
                for t in range(tiles):
                    field[2 * s + c, group, t, inner : inner + rows_here, :] = recv[
                        s, p, c * rows_here : (c + 1) * rows_here, t * LANES : (t + 1) * LANES
                    ]

    bin_here = (lowest_bin + me * cores + core).astype(jnp.float32)
    per_slow = top_wavenumber * bin_here / (lowest_bin + bin_count)

    def coefficients(z, chunk):
        wavenumber = per_slow * slow_t[z * chunks + chunk]
        squared = wavenumber * wavenumber
        pairs = [node_value(squared, angle) for angle in NODE_ANGLES]
        for comp in range(2):
            found = project([pair[comp] for pair in pairs], list(range(NTERMS)), NODES)
            for term in range(NTERMS):
                coef[z][2 * term + comp, chunk] = found[term]

    def all_coefficients(z):
        if inline:
            for chunk in range(chunks):
                coefficients(z, chunk)
        else:
            lax.fori_loop(0, chunks, lambda chunk, carry: coefficients(z, chunk) or carry, 0)

    all_coefficients(0)

    shape = (1, 1, 1, SUBLANES, LANES)
    lane = lax.broadcasted_iota(jnp.int32, shape, 4)
    row = lax.broadcasted_iota(jnp.int32, shape, 3)
    values = field[...]
    half_groups = groups // 2
    image_copies = []
    for z in range(depths):

        def term_of(current, n):
            here = coef[z][pl.ds(2 * n, 2)]
            real_c = here[0].reshape(groups, tiles, SUBLANES, LANES)
            imag_c = here[1].reshape(groups, tiles, SUBLANES, LANES)
            return jnp.stack(
                [
                    real_c * current[0] - imag_c * current[1],
                    real_c * current[1] + imag_c * current[0],
                    real_c * current[2] + imag_c * current[3],
                    real_c * current[3] - imag_c * current[2],
                ]
            )

        first = 0.5 * spread_twice(values, lane, row) - values
        summed = term_of(values, 0) + term_of(first, 1)

        def advance(n, state):
            previous, current, total = state
            following = spread_twice(current, lane, row) - (2.0 * current + previous)
            return current, following, total + term_of(following, n)

        state = (values, first, summed)
        if inline:
            for n in range(2, NTERMS):
                state = advance(n, state)
                if z + 1 < depths and n % 2 == 0 and n // 2 <= chunks:
                    coefficients(z + 1, n // 2 - 1)
        else:
            state = lax.fori_loop(2, NTERMS, advance, state)
            if z + 1 < depths:
                all_coefficients(z + 1)
        values = state[2]
        picture = values[0] * values[2] + values[1] * values[3]
        for group in range(groups):
            for t in range(tiles):
                image[z, group // half_groups,
                      (group % half_groups) * SUBLANES : (group % half_groups + 1) * SUBLANES,
                      t * LANES : (t + 1) * LANES] = picture[group, t]
        other = lax.rem(core + 1, cores)
        copy = pltpu.make_async_remote_copy(
            src_ref=image.at[z, other], dst_ref=out_ref.at[core, z],
            send_sem=image_send.at[z], recv_sem=image_recv.at[z],
            device_id={"field": other}, device_id_type=pl.DeviceIdType.MESH,
        )
        copy.start()
        image_copies.append(copy)
        out_ref[core, z] = image[z, core]
    for copy in spec_copies:
        copy.wait_send()
    for copy in image_copies:
        copy.wait()


def local(traces, slowness):
    peers, cores = lax.axis_size("freq"), lax.axis_size("field")
    _, length, rows_here, cols = traces.shape
    depths = slowness.shape[0]
    bin_count = peers * cores
    table = jnp.asarray(dft_rows(bin_count, length, peers, cores, rows_here))
    grid_rows = peers * rows_here
    groups, tiles = grid_rows // SUBLANES, cols // LANES
    f32 = jnp.float32
    others = peers * cores - 1
    return pl.pallas_call(
        functools.partial(kernel, peers, cores, depths, rows_here, bin_count, cols),
        out_shape=jax.ShapeDtypeStruct((cores, depths, grid_rows // 2, cols), f32),
        in_specs=[pl.BlockSpec(memory_space=pltpu.HBM)] * 3,
        out_specs=pl.BlockSpec(memory_space=pltpu.VMEM),
        scratch_shapes=[
            pltpu.VMEM((length, rows_here, cols), jnp.bfloat16),
            pltpu.VMEM(table.shape, jnp.bfloat16),
            pltpu.VMEM((depths, rows_here, cols), f32),
            pltpu.VMEM((peers, cores, (2 + depths) * rows_here, cols), f32),
            pltpu.VMEM((cores, peers, (2 + depths) * rows_here, cols), f32),
            pltpu.VMEM((depths * groups * tiles, SUBLANES, LANES), f32),
            pltpu.VMEM((4, groups, tiles, SUBLANES, LANES), f32),
            pltpu.VMEM((depths, 2, grid_rows // 2, cols), f32),
            pltpu.SemaphoreType.DMA((2 + PIECES,)),
            pltpu.SemaphoreType.DMA((others,)),
            pltpu.SemaphoreType.DMA((others,)),
            pltpu.SemaphoreType.DMA((depths,)),
            pltpu.SemaphoreType.DMA((depths,)),
        ]
        + [pltpu.VMEM((2 * NTERMS, groups * tiles, SUBLANES, LANES), f32)] * depths,
        compiler_params=pltpu.CompilerParams(
            collective_id=0, has_side_effects=True, vmem_limit_bytes=64 * 1024 * 1024
        ),
    )(traces[0], table, slowness)


def solution(mesh):
    return jax.shard_map(
        local,
        mesh=mesh,
        in_specs=(P("field", None, ("shot", "freq"), None), P("shot", "freq", None)),
        out_specs=P(("shot", "freq"), None, "field", None),
        check_vma=False,
    )
```
